32 devices in a mesh: grp: 4 (over y, x), mdl: 8 (over z, core).
Axes of the slice: x: 2, y: 2, z: 4, core: 2. Of those that a mesh axis runs over, the one named last changes fastest.
Arguments:
- pol_hidden: bfloat16 [128, 4096], P(('grp', 'mdl')), may hold values from -6 to 6
- ref_hidden: bfloat16 [128, 4096], P(('grp', 'mdl')), may hold values from -6 to 6
- pol_mlp_gain: bfloat16 [4096], replicated, may hold values from 0.099609375 to 1.8984375
- ref_mlp_gain: bfloat16 [4096], replicated, may hold values from 0.099609375 to 1.8984375
- pol_final_gain: bfloat16 [4096], replicated, may hold values from 0.099609375 to 1.8984375
- ref_final_gain: bfloat16 [4096], replicated, may hold values from 0.099609375 to 1.8984375
- pol_gate: bfloat16 [4096, 11008], P(None, 'mdl'), may hold values from -0.09375 to 0.09375
- pol_up: bfloat16 [4096, 11008], P(None, 'mdl'), may hold values from -0.09375 to 0.09375
- pol_down: bfloat16 [11008, 4096], P('mdl'), may hold values from -0.109375 to 0.109375
- ref_gate: bfloat16 [4096, 11008], P(None, 'mdl'), may hold values from -0.09375 to 0.09375
- ref_up: bfloat16 [4096, 11008], P(None, 'mdl'), may hold values from -0.09375 to 0.09375
- ref_down: bfloat16 [11008, 4096], P('mdl'), may hold values from -0.109375 to 0.109375
- pol_head: bfloat16 [64000, 4096], P(('grp', 'mdl')), may hold values from -20 to 20
- ref_head: bfloat16 [64000, 4096], P(('grp', 'mdl')), may hold values from -20 to 20
- token_ids: int32 [128], replicated, may hold values from 0 to 63999
- lengths: int32 [16], replicated, may hold values from 1 to 32, 128 in all
Outputs:
- pol_out: bfloat16 [128, 4096], P(('grp', 'mdl'))
- ref_out: bfloat16 [128, 4096], P(('grp', 'mdl'))
- rollout_ratio: float32 [16], replicated
The draws below stay inside these ranges and needn't reach their ends.
Inputs may be any that keep to these rules, and one draw needn't show every extreme that they name: Rollout lengths sum to 128; the longest is exactly 32.
All inputs are finite; a program needn't handle non-finite values.
Results may differ from the reference program's by a relative error of at most 0.012.
The reference program's roundings to bfloat16 on the way count: a program that leaves them out, or rounds other values in their place, can miss the bound.
Values may be sent and summed in bfloat16 or wider, within the bound.
A program may use at most 192 MiB of HBM per device.

```python
import math
import jax
import jax.numpy as jnp
import numpy as np
from jax import lax

D = 4096
FF = 11008
V = 64000
R = 16
TOKENS = 128
LEN_MAX = 32
N_GRP = 4


def head_rows(key):
    first = jax.random.fold_in(key, 0)
    base = jnp.clip(jax.random.normal(first, (V, D), jnp.float32), -6.0, 6.0) * (3.0 / math.sqrt(D))
    return jnp.clip(base, -20.0, 20.0)


def draw_pol_head(key, part):
    return head_rows(jax.random.fold_in(key, 11)).astype(jnp.bfloat16)


def draw_ref_head(key, part):
    return head_rows(jax.random.fold_in(key, 23)).astype(jnp.bfloat16)


def with_ends(drawn, key, least, largest):
    shape = drawn.shape
    place = [jax.random.randint(jax.random.fold_in(key, axis), (), 0, shape[axis]) for axis in range(len(shape))]
    drawn = drawn.at[tuple(place)].set(least)
    longest = shape.index(max(shape))
    place[longest] = (place[longest] + 1) % shape[longest]
    return drawn.at[tuple(place)].set(largest)


def block_scale(stream_key, shape, cuts, least, high):
    factor_of, own = 1.0, jax.random.fold_in(stream_key, 6)
    for axis_at, blocks in cuts:
        draws = jnp.exp(jax.random.uniform(jax.random.fold_in(own, axis_at), (blocks,), jnp.float32, least / len(cuts), high / len(cuts)))
        factor_of = factor_of * jnp.repeat(draws, shape[axis_at] // blocks).reshape([-1 if axis == axis_at else 1 for axis in range(len(shape))])
    return factor_of


def split_up(amount, total, limit, slope):
    portions = [(1 << 20) // math.isqrt(rank ** slope) + 1 for rank in range(2, amount + 1)]
    rest, holding = total - limit - (amount - 1), [1] * (amount - 1)
    while rest > 0:
        free = [i for i in range(amount - 1) if holding[i] < limit]
        pool, budget = sum([portions[i] for i in free]), rest
        for i in free:
            addition = min(limit - holding[i], max(1, budget * portions[i] // pool), rest)
            holding[i] = holding[i] + addition
            rest = rest - addition
    return np.array([limit] + holding)


def uneven_parts(stream_key, number_of, total, limit, skew):
    if number_of == 2:
        one = jax.random.randint(stream_key, (), max(1, total - limit), min(limit, total - 1) + 1)
        return jnp.stack([one, total - one])
    sizes = jnp.asarray(split_up(number_of, total, limit, skew), jnp.int32)
    twos = (number_of - 1) // 2
    donor, sink = sizes[1:1 + 2 * twos:2], sizes[2:2 + 2 * twos:2]
    slack = jnp.minimum(donor - 1, limit - sink)
    passed = jax.random.randint(jax.random.fold_in(stream_key, 1), (twos,), 0, 1 << 20) % (slack + 1)
    sizes = sizes.at[1:1 + 2 * twos:2].set(donor - passed).at[2:2 + 2 * twos:2].set(sink + passed)
    return sizes[jax.random.permutation(jax.random.fold_in(stream_key, 2), number_of)]


def normal_values(key, extent, spread, limit, shards=(), kind=jnp.bfloat16):
    level = block_scale(key, extent, shards, -0.22, 0.18) if shards else 1.0
    array = jax.random.normal(key, extent, jnp.float32) * spread * level
    return jnp.minimum(jnp.maximum(array, -limit), limit).astype(kind)


def setup_inputs(seed: int = 0) -> dict:
    seeds = jax.random.split(jax.random.key(seed), 17)
    pol_hidden = normal_values(seeds[0], (TOKENS, D), 1.0, 6.0, ((0, 32),))
    ref_hidden = normal_values(seeds[1], (TOKENS, D), 1.0, 6.0, ((0, 32),))
    pol_mlp_gain = jnp.clip(1.0 + 0.18 * jax.random.normal(seeds[2], (D,), jnp.float32), 0.099609375, 1.8984375).astype(jnp.bfloat16)
    ref_mlp_gain = jnp.clip(1.0 + 0.18 * jax.random.normal(seeds[3], (D,), jnp.float32), 0.099609375, 1.8984375).astype(jnp.bfloat16)
    pol_final_gain = jnp.clip(1.0 + 0.18 * jax.random.normal(seeds[4], (D,), jnp.float32), 0.099609375, 1.8984375).astype(jnp.bfloat16)
    ref_final_gain = jnp.clip(1.0 + 0.18 * jax.random.normal(seeds[5], (D,), jnp.float32), 0.099609375, 1.8984375).astype(jnp.bfloat16)
    pol_gate = normal_values(seeds[6], (D, FF), D ** -0.5, 0.09375, ((1, 8),))
    pol_up = normal_values(seeds[7], (D, FF), D ** -0.5, 0.09375, ((1, 8),))
    pol_down = normal_values(seeds[8], (FF, D), (FF // 4) ** -0.5, 0.109375, ((0, 8),))
    ref_gate = normal_values(seeds[9], (D, FF), D ** -0.5, 0.09375, ((1, 8),))
    ref_up = normal_values(seeds[10], (D, FF), D ** -0.5, 0.09375, ((1, 8),))
    ref_down = normal_values(seeds[11], (FF, D), (FF // 4) ** -0.5, 0.109375, ((0, 8),))
    pol_head = draw_pol_head(jax.random.fold_in(seeds[16], 71), 0)
    ref_head = draw_ref_head(jax.random.fold_in(seeds[16], 71), 0)
    token_ids = with_ends(jax.random.randint(seeds[14], (TOKENS,), 0, V), jax.random.fold_in(seeds[14], 1), 0, V - 1).astype(jnp.int32)
    lengths = uneven_parts(seeds[15], R, TOKENS, LEN_MAX, 2).astype(jnp.int32)
    return {"pol_hidden": pol_hidden, "ref_hidden": ref_hidden, "pol_mlp_gain": pol_mlp_gain, "ref_mlp_gain": ref_mlp_gain, "pol_final_gain": pol_final_gain, "ref_final_gain": ref_final_gain, "pol_gate": pol_gate, "pol_up": pol_up, "pol_down": pol_down, "ref_gate": ref_gate, "ref_up": ref_up, "ref_down": ref_down, "pol_head": pol_head, "ref_head": ref_head, "token_ids": token_ids, "lengths": lengths}


def rms_rows(rows, gain):
    values = rows.astype(jnp.float32)
    scale = lax.rsqrt(lax.optimization_barrier(jnp.mean(values * values, axis=-1, keepdims=True)) + 1e-05)
    return (values * scale * gain.astype(jnp.float32)).astype(jnp.bfloat16)

def sublayer(hidden_in, gain, w_gate, w_up, w_down):
    normed = rms_rows(hidden_in, gain)
    gate = jnp.dot(normed, w_gate, preferred_element_type=jnp.float32)
    upper = jnp.dot(normed, w_up, preferred_element_type=jnp.float32)
    hidden = (jax.nn.silu(gate) * upper).astype(jnp.bfloat16)
    mixed = jnp.dot(hidden, w_down, preferred_element_type=jnp.float32)
    return (hidden_in.astype(jnp.float32) + mixed).astype(jnp.bfloat16)

def log_probs(final, head, token_ids):

    def one_block(pair):
        block_rows, block_targets = pair
        logits = jnp.dot(block_rows, head.T, preferred_element_type=jnp.float32)
        peak = lax.optimization_barrier(jnp.max(logits, axis=1))
        total = lax.optimization_barrier(jnp.sum(jnp.exp(logits - peak[:, None]), axis=1))
        picked = jnp.take_along_axis(logits, block_targets[:, None], axis=1)[:, 0]
        return picked - peak - jnp.log(total)
    return lax.map(one_block, (final.reshape(N_GRP, -1, D), token_ids.reshape(N_GRP, -1))).reshape(-1)

def reference(pol_hidden, ref_hidden, pol_mlp_gain, ref_mlp_gain, pol_final_gain, ref_final_gain, pol_gate, pol_up, pol_down, ref_gate, ref_up, ref_down, pol_head, ref_head, token_ids, lengths):
    pol_out = sublayer(pol_hidden, pol_mlp_gain, pol_gate, pol_up, pol_down)
    ref_out = sublayer(ref_hidden, ref_mlp_gain, ref_gate, ref_up, ref_down)
    pol_logp = log_probs(rms_rows(pol_out, pol_final_gain), pol_head, token_ids)
    ref_logp = log_probs(rms_rows(ref_out, ref_final_gain), ref_head, token_ids)
    ends = jnp.cumsum(lengths).astype(jnp.int32)
    positions = jnp.arange(TOKENS, dtype=jnp.int32)
    owner = lax.optimization_barrier(jnp.sum((positions[:, None] >= ends[None, :]).astype(jnp.int32), axis=1))
    onehot = (owner[:, None] == jnp.arange(R, dtype=jnp.int32)[None, :]).astype(jnp.float32)
    log_ratio = pol_logp - ref_logp
    rollout_ratio = lax.optimization_barrier(jnp.sum(log_ratio[:, None] * onehot, axis=0))
    return (pol_out, ref_out, rollout_ratio)
```

```python
import functools

import jax
import jax.numpy as jnp
from jax import lax
from jax.experimental import pallas as pl
from jax.experimental.pallas import tpu as pltpu
from jax.sharding import PartitionSpec as P

MESH = pl.DeviceIdType.MESH
DEPTH = 4
EARLY = 2
VMEM_LIMIT = 62 * 1024 * 1024


def rms_rows(rows, gain):
    values = rows.astype(jnp.float32)
    scale = lax.rsqrt(jnp.mean(values * values, axis=-1, keepdims=True) + 1e-05)
    return (values * scale * gain.astype(jnp.float32)).astype(jnp.bfloat16)


def mlp_hidden(piece, gain, w_gate, w_up):
    normed = rms_rows(piece, gain)
    gate = jnp.dot(normed, w_gate, preferred_element_type=jnp.float32)
    upper = jnp.dot(normed, w_up, preferred_element_type=jnp.float32)
    return (jax.nn.silu(gate) * upper).astype(jnp.bfloat16)


def vocab_terms(token_rows, head_rows, targets, vocab):
    logits = jnp.einsum("td,vd->tv", token_rows, head_rows, preferred_element_type=jnp.float32)
    peak = jnp.max(logits, axis=1)
    total = jnp.sum(jnp.exp(logits - peak[:, None]), axis=1)
    target = jnp.sum(jnp.where(targets[:, None] == vocab[None, :], logits, 0.0), axis=1)
    return (peak, total, target)


def rollout_totals(log_ratio, positions, lengths):
    order = jnp.arange(lengths.shape[0], dtype=jnp.int32)
    ends = jnp.sum(jnp.where(order[None, :] <= order[:, None], lengths[None, :], 0), axis=1)
    owner = jnp.sum((positions[:, None] >= ends[None, :]).astype(jnp.int32), axis=1)
    onehot = (owner[:, None] == jnp.arange(lengths.shape[0], dtype=jnp.int32)[None, :]).astype(
        jnp.float32
    )
    return jnp.sum(log_ratio[:, None] * onehot, axis=0)


def per_device(
    pol_hidden,
    ref_hidden,
    pol_mlp_gain,
    ref_mlp_gain,
    pol_final_gain,
    ref_final_gain,
    pol_gate,
    pol_up,
    pol_down,
    ref_gate,
    ref_up,
    ref_down,
    pol_head,
    ref_head,
    token_ids,
    lengths,
):
    results = []
    models = (
        (pol_hidden, pol_mlp_gain, pol_gate, pol_up, pol_down),
        (ref_hidden, ref_mlp_gain, ref_gate, ref_up, ref_down),
    )
    for hidden_in, gain, w_gate, w_up, w_down in models:

        def expand(piece, start, gain=gain, w_gate=w_gate, w_up=w_up):
            return mlp_hidden(piece, gain, w_gate, w_up)

        hidden = expand(lax.all_gather(hidden_in, "mdl", axis=0, tiled=True), jnp.int32(0))

        def project(start, count, hidden=hidden, w_down=w_down):
            return jnp.dot(hidden, w_down, preferred_element_type=jnp.float32)

        mixed = lax.psum_scatter(
            project(jnp.int32(0), hidden_in.shape[0] * lax.axis_size("mdl")),
            "mdl",
            scatter_dimension=0,
            tiled=True,
        )
        results.append((hidden_in.astype(jnp.float32) + mixed).astype(jnp.bfloat16))
    finals = [rms_rows(results[0], pol_final_gain), rms_rows(results[1], ref_final_gain)]
    voc_dev = pol_head.shape[0]
    members = lax.axis_size("mdl")
    group = lax.axis_index("grp")
    member = lax.axis_index("mdl")
    pol_rows, ref_rows = (
        lax.all_gather(finals[0], ("grp", "mdl"), axis=0, tiled=True),
        lax.all_gather(finals[1], ("grp", "mdl"), axis=0, tiled=True),
    )
    positions = jnp.arange(pol_rows.shape[0], dtype=jnp.int32)
    vocab = (group * members + member) * voc_dev + jnp.arange(voc_dev, dtype=jnp.int32)
    pol_terms = vocab_terms(pol_rows, pol_head, token_ids, vocab)
    ref_terms = vocab_terms(ref_rows, ref_head, token_ids, vocab)
    peaks = lax.pmax((pol_terms[0], ref_terms[0]), ("grp", "mdl"))
    sums = lax.psum(
        (
            pol_terms[1] * jnp.exp(pol_terms[0] - peaks[0]),
            pol_terms[2],
            ref_terms[1] * jnp.exp(ref_terms[0] - peaks[1]),
            ref_terms[2],
        ),
        ("grp", "mdl"),
    )
    pol_logp = sums[1] - peaks[0] - jnp.log(sums[0])
    ref_logp = sums[3] - peaks[1] - jnp.log(sums[2])
    rollout_ratio = rollout_totals(pol_logp - ref_logp, positions, lengths)
    return (results[0], results[1], rollout_ratio)


def fused_kernel(
    n_grp, n_mdl, n_k, n_head,
    pol_hid, ref_hid, pol_mg, ref_mg, pol_fg, ref_fg,
    pol_gate, pol_up, pol_down, ref_gate, ref_up, ref_down,
    pol_head, ref_head, ids, lengths,
    pol_out, ref_out, ratio_out,
    hid, xs, xraw, acc_g, acc_u, hbuf, ring_a, ring_b, heads,
    rs_send, rs_recv, own_part, yall, fin, st_send, st1, st2,
    sem_a, sem_b, sem_h, hs_sem, hr_sem, rss_sem, rsr_sem,
    zs_sem, xs_sem, cs_sem, yr_sem, s1s_sem, s1r_sem, s2s_sem, s2r_sem,
):
    g = lax.axis_index("grp")
    m = lax.axis_index("mdl")
    n_z = n_mdl // 2
    tg = xs.shape[2]
    kc = xs.shape[3]
    d = pol_gate.shape[0]
    cb = d // n_mdl
    quarter = d // 4
    hc = pol_head.shape[0] // n_head
    gates, ups, downs = (pol_gate, ref_gate), (pol_up, ref_up), (pol_down, ref_down)
    head_refs = (pol_head, ref_head)
    hids, mgs, fgs = (pol_hid, ref_hid), (pol_mg, ref_mg), (pol_fg, ref_fg)
    outs = (pol_out, ref_out)

    def copy_a(mod, k):
        slot = lax.rem(k, DEPTH) * 2
        rows = pl.ds(pl.multiple_of(k * kc, kc), kc)
        return (
            pltpu.make_async_copy(gates[mod].at[rows, :], ring_a.at[slot], sem_a.at[slot]),
            pltpu.make_async_copy(ups[mod].at[rows, :], ring_a.at[slot + 1], sem_a.at[slot + 1]),
        )

    def start_a(mod, k):
        for c in copy_a(mod, k):
            c.start()

    def copy_b(mod, j):
        peer = lax.rem(m + 1 + j, n_mdl)
        cols = pl.ds(pl.multiple_of(peer * cb, cb), cb)
        return pltpu.make_async_copy(downs[mod].at[:, cols], ring_b.at[j], sem_b.at[j])

    def copy_h(mod, c):
        rows = pl.ds(pl.multiple_of(c * hc, hc), hc)
        return pltpu.make_async_copy(head_refs[mod].at[rows, :], heads.at[mod, c], sem_h.at[mod, c])

    def remote(src, dst, ssem, rsem, dg, dm):
        return pltpu.make_async_remote_copy(
            src_ref=src, dst_ref=dst, send_sem=ssem, recv_sem=rsem,
            device_id=(dg, dm), device_id_type=MESH,
        )

    def loop(n, body, start=0):
        def step(i, carry):
            body(i)
            return carry

        lax.fori_loop(start, n, step, 0)

    loop(DEPTH, lambda k: start_a(0, k))
    loop(n_mdl, lambda j: copy_b(0, j).start())
    loop(EARLY, lambda c: copy_h(0, c).start())

    barrier = pltpu.get_barrier_semaphore()
    for i in range(1, n_mdl):
        pl.semaphore_signal(barrier, inc=1, device_id=(g, lax.rem(m + i, n_mdl)), device_id_type=MESH)
    for i in range(1, n_grp):
        pl.semaphore_signal(barrier, inc=1, device_id=(lax.rem(g + i, n_grp), m), device_id_type=MESH)
    pl.semaphore_wait(barrier, n_mdl + n_grp - 2)

    def hid_rows(mod, who):
        return hid.at[mod, pl.ds(pl.multiple_of(who * 16, 16), 16)]

    def hid_copy(mod, i, sender):
        peer = lax.rem(m + 1 + i, n_mdl)
        return remote(hids[mod], hid_rows(mod, sender), hs_sem.at[mod, i], hr_sem.at[mod, sender], g, peer)

    for mod in (0, 1):
        loop(n_mdl - 1, lambda i, mod=mod: hid_copy(mod, i, m).start())
        hid[mod, pl.ds(pl.multiple_of(m * 16, 16), 16)] = hids[mod][...]

    def normed_input(mod):
        loop(n_mdl - 1, lambda i: hid_copy(mod, i, lax.rem(m + 1 + i, n_mdl)).wait_recv())
        stacked = hid[mod]
        t = lax.broadcasted_iota(jnp.int32, (tg, n_mdl * 16), 0)
        r = lax.broadcasted_iota(jnp.int32, (tg, n_mdl * 16), 1)
        parts = []
        total = jnp.zeros((tg, 1), jnp.float32)
        for q in range(4):
            pick = (r == t * 4 + q).astype(jnp.bfloat16)
            part = jnp.dot(pick, stacked, preferred_element_type=jnp.float32)
            total += jnp.sum(part * part, axis=1, keepdims=True)
            parts.append(part)
        scale = lax.rsqrt(total / d + 1e-05)
        for q in range(4):
            gain = mgs[mod][:, q * quarter:(q + 1) * quarter].astype(jnp.float32)
            normed = (parts[q] * scale * gain).astype(jnp.bfloat16)
            raw = parts[q].astype(jnp.bfloat16)
            for b in range(quarter // kc):
                xs[mod, q * (quarter // kc) + b] = normed[:, b * kc:(b + 1) * kc]
            for b in range(quarter // cb):
                xraw[mod, q * (quarter // cb) + b] = raw[:, b * cb:(b + 1) * cb]

    def expand_step(mod, k, first):
        for c in copy_a(mod, k):
            c.wait()
        slot = lax.rem(k, DEPTH) * 2
        rows = xs[mod, k]
        acc_g[...] += jnp.dot(rows, ring_a[slot], preferred_element_type=jnp.float32)
        acc_u[...] += jnp.dot(rows, ring_a[slot + 1], preferred_element_type=jnp.float32)

    def expand(mod):
        acc_g[...] = jnp.zeros_like(acc_g)
        acc_u[...] = jnp.zeros_like(acc_u)

        def early(k):
            expand_step(mod, k, None)
            start_a(mod, k + DEPTH)

        loop(n_k - DEPTH, early)

        def late(k):
            expand_step(mod, k, None)
            if mod == 0:
                start_a(1, k - (n_k - DEPTH))

        loop(n_k, late, n_k - DEPTH)
        gate = acc_g[...]
        hbuf[...] = (gate / (1.0 + jnp.exp(-gate)) * acc_u[...]).astype(jnp.bfloat16)

    def rs_copy(mod, i, sender):
        peer = lax.rem(m + 1 + i, n_mdl)
        return remote(rs_send.at[mod, i], rs_recv.at[mod, sender], rss_sem.at[mod, i],
                      rsr_sem.at[mod, sender], g, peer)

    def project(mod):
        def part(j):
            copy_b(mod, j).wait()
            return jnp.dot(hbuf[...], ring_b[j], preferred_element_type=jnp.float32)

        def step(j):
            rs_send[mod, j] = part(j).astype(jnp.bfloat16)
            rs_copy(mod, j, m).start()
            if mod == 0:
                copy_b(1, j).start()

        loop(n_mdl - 1, step)
        own_part[mod] = part(n_mdl - 1)
        if mod == 0:
            copy_b(1, n_mdl - 1).start()

    core = lax.rem(m, 2)
    sibling = m + 1 - 2 * core
    me = g * n_mdl + m

    def z_peer(i):
        return lax.rem(m + 2 * i, n_mdl)

    def z_copy(mod, i, block):
        return remote(yall.at[mod, block], yall.at[mod, block], zs_sem.at[mod, i], yr_sem.at[mod, block],
                      g, z_peer(i + 1))

    def x_copy(mod, zi, i, block):
        return remote(yall.at[mod, block], yall.at[mod, block], xs_sem.at[mod, zi, i], yr_sem.at[mod, block],
                      lax.rem(g + 1 + i, n_grp), m)

    def c_copy(mod, gi, zi, block):
        return remote(yall.at[mod, block], yall.at[mod, block], cs_sem.at[mod, gi, zi], yr_sem.at[mod, block],
                      g, sibling)

    def block_of(gi, zi):
        return lax.rem(g + gi, n_grp) * n_mdl + z_peer(zi)

    def finish(mod):
        total = own_part[mod] + xraw[mod, m].astype(jnp.float32)
        for i in range(n_mdl - 1):
            sender = lax.rem(m + 1 + i, n_mdl)
            rs_copy(mod, i, sender).wait_recv()
            total += rs_recv[mod, sender].astype(jnp.float32)
        yall[mod, me] = total.astype(jnp.bfloat16)
        loop(n_z - 1, lambda i: z_copy(mod, i, me).start())
        loop(n_grp - 1, lambda i: x_copy(mod, 0, i, me).start())
        c_copy(mod, 0, 0, me).start()

    def spread_grp(mod):
        def step(zi):
            block = block_of(0, zi)
            z_copy(mod, zi - 1, block).wait_recv()
            loop(n_grp - 1, lambda i: x_copy(mod, zi, i, block).start())
            c_copy(mod, 0, zi, block).start()

        loop(n_z, step, 1)

    def spread_core(mod):
        def per_z(zi):
            def per_g(gi):
                block = block_of(gi, zi)
                x_copy(mod, zi, gi - 1, block).wait_recv()
                c_copy(mod, gi, zi, block).start()

            loop(n_grp, per_g, 1)

        loop(n_z, per_z)

    def arrive(mod):
        def per_z(zi):
            def per_g(gi):
                block = lax.rem(g + gi, n_grp) * n_mdl + lax.rem(sibling + 2 * zi, n_mdl)
                c_copy(mod, gi, zi, block).wait_recv()

            loop(n_grp, per_g)

        loop(n_z, per_z)

    def final_norm(mod):
        for gi in range(n_grp):
            total = jnp.zeros((tg, 1), jnp.float32)
            for b in range(n_mdl):
                y = yall[mod, gi * n_mdl + b].astype(jnp.float32)
                total += jnp.sum(y * y, axis=1, keepdims=True)
            scale = lax.rsqrt(total / d + 1e-05)
            for b in range(n_mdl):
                y = yall[mod, gi * n_mdl + b].astype(jnp.float32)
                gain = fgs[mod][:, b * cb:(b + 1) * cb].astype(jnp.float32)
                fin[gi * tg:(gi + 1) * tg, b * cb:(b + 1) * cb] = (y * scale * gain).astype(jnp.bfloat16)

    def write_out(mod):
        rows = outs[mod].shape[0]
        r = lax.broadcasted_iota(jnp.int32, (8, tg), 0)
        t = lax.broadcasted_iota(jnp.int32, (8, tg), 1)
        pick = (t == m * rows + r).astype(jnp.bfloat16)
        for b in range(n_mdl):
            got = jnp.dot(pick, yall[mod, g * n_mdl + b], preferred_element_type=jnp.float32)
            outs[mod][:, b * cb:(b + 1) * cb] = got[:rows].astype(jnp.bfloat16)

    tokens = fin.shape[0]
    first_word = me * (hc * n_head)

    def head_step(mod, c, carry):
        peak, total, target = carry
        copy_h(mod, c).wait()
        logits = lax.dot_general(heads[mod, c], fin[...], (((1,), (1,)), ((), ())),
                                 preferred_element_type=jnp.float32)
        higher = jnp.maximum(peak, jnp.max(logits, axis=0, keepdims=True))
        total = total * jnp.exp(peak - higher) + jnp.sum(jnp.exp(logits - higher), axis=0, keepdims=True)
        word = lax.broadcasted_iota(jnp.int32, (hc, tokens), 0) + (first_word + c * hc)
        target = target + jnp.sum(jnp.where(word == ids[...], logits, 0.0), axis=0, keepdims=True)
        return (higher, total, target)

    def head_part(mod, lo, hi, carry):
        return lax.fori_loop(lo, hi, lambda c, carry: head_step(mod, c, carry), carry)

    def nothing():
        return (
            jnp.full((1, tokens), -3.0e38, jnp.float32),
            jnp.zeros((1, tokens), jnp.float32),
            jnp.zeros((1, tokens), jnp.float32),
        )

    normed_input(0)
    expand(0)
    project(0)
    normed_input(1)
    loop(n_head, lambda c: copy_h(0, c).start(), EARLY)
    expand(1)
    loop(n_head, lambda c: copy_h(1, c).start())
    finish(0)
    project(1)
    spread_grp(0)
    spread_core(0)
    finish(1)
    arrive(0)
    final_norm(0)
    spread_grp(1)
    stats = head_part(0, 0, 3, nothing())
    spread_core(1)
    pol = head_part(0, 3, n_head, stats)
    write_out(0)
    arrive(1)
    final_norm(1)
    ref = head_part(1, 0, n_head, nothing())

    for row, value in enumerate(pol + ref):
        st_send[0, row:row + 1, :] = value
        st1[m, row:row + 1, :] = value

    def s1_copy(i, sender):
        return remote(st_send.at[0], st1.at[sender], s1s_sem.at[i], s1r_sem.at[sender],
                      g, lax.rem(m + 1 + i, n_mdl))

    def s2_copy(i, sender):
        return remote(st_send.at[1], st2.at[sender], s2s_sem.at[i], s2r_sem.at[sender],
                      lax.rem(g + 1 + i, n_grp), m)

    def merge(ref, count):
        merged = []
        for base in (0, 3):
            peaks = [ref[i, base:base + 1, :] for i in range(count)]
            peak = functools.reduce(jnp.maximum, peaks)
            total = jnp.zeros((1, tokens), jnp.float32)
            target = jnp.zeros((1, tokens), jnp.float32)
            for i in range(count):
                total += ref[i, base + 1:base + 2, :] * jnp.exp(peaks[i] - peak)
                target += ref[i, base + 2:base + 3, :]
            merged += [peak, total, target]
        return merged

    loop(n_mdl - 1, lambda i: s1_copy(i, m).start())
    write_out(1)
    loop(n_mdl - 1, lambda i: s1_copy(i, lax.rem(m + 1 + i, n_mdl)).wait_recv())
    for row, value in enumerate(merge(st1, n_mdl)):
        st_send[1, row:row + 1, :] = value
        st2[g, row:row + 1, :] = value
    loop(n_grp - 1, lambda i: s2_copy(i, g).start())

    for mod in (0, 1):
        loop(n_mdl - 1, lambda i, mod=mod: hid_copy(mod, i, m).wait_send())
        loop(n_mdl - 1, lambda i, mod=mod: rs_copy(mod, i, m).wait_send())
        loop(n_z - 1, lambda i, mod=mod: z_copy(mod, i, me).wait_send())

        def sent(zi, mod=mod):
            loop(n_grp - 1, lambda i: x_copy(mod, zi, i, block_of(0, zi)).wait_send())
            loop(n_grp, lambda gi: c_copy(mod, gi, zi, block_of(gi, zi)).wait_send())

        loop(n_z, sent)
    loop(n_mdl - 1, lambda i: s1_copy(i, m).wait_send())

    n_roll = ratio_out.shape[0]
    row = lax.broadcasted_iota(jnp.int32, (n_roll, n_roll), 0)
    col = lax.broadcasted_iota(jnp.int32, (n_roll, n_roll), 1)
    size = jnp.broadcast_to(lengths[...].astype(jnp.float32), (n_roll, n_roll))
    ends = jnp.sum(jnp.where(col <= row, size, 0.0), axis=1, keepdims=True)
    starts = jnp.sum(jnp.where(col < row, size, 0.0), axis=1, keepdims=True)
    position = lax.broadcasted_iota(jnp.int32, (n_roll, tokens), 1).astype(jnp.float32)
    held = jnp.where((position >= starts) & (position < ends), 1.0, 0.0)

    loop(n_grp - 1, lambda i: s2_copy(i, lax.rem(g + 1 + i, n_grp)).wait_recv())
    pp, ps, pt, rp, rt, rg = merge(st2, n_grp)
    log_ratio = (pt - pp - jnp.log(ps)) - (rg - rp - jnp.log(rt))
    ratio_out[...] = jnp.sum(held * log_ratio, axis=1, keepdims=True)
    loop(n_grp - 1, lambda i: s2_copy(i, g).wait_send())


def pick_head_chunks(voc):
    for n in (5, 4, 8, 10):
        if voc % n == 0 and (voc // n) % 16 == 0:
            return n
    return 0


def fits(n_grp, n_mdl, rows, d, ff, voc, tokens):
    if rows != 4 or n_mdl % 2 or n_mdl < 4 or n_grp < 2 or tokens > 128 or not pick_head_chunks(voc):
        return False
    if d % (4 * n_mdl) or (d // n_mdl) % 128 or d % 32 or (d // 8) % 128 or (d // 4) % (d // n_mdl) or ff % 16:
        return False
    need = 2 * (2 * DEPTH * (d // 8) * ff + ff * d + 2 * voc * d + 6 * tokens * d)
    return need < VMEM_LIMIT


def fused(
    pol_hidden, ref_hidden, pol_mlp_gain, ref_mlp_gain, pol_final_gain, ref_final_gain,
    pol_gate, pol_up, pol_down, ref_gate, ref_up, ref_down, pol_head, ref_head, token_ids, lengths,
):
    n_grp, n_mdl = lax.axis_size("grp"), lax.axis_size("mdl")
    rows, d = pol_hidden.shape
    ff, voc, tokens = pol_gate.shape[1], pol_head.shape[0], token_ids.shape[0]
    n_k, n_head = 8, pick_head_chunks(voc)
    tg, kc, cb, hc = rows * n_mdl, d // n_k, d // n_mdl, voc // n_head
    n_z = n_mdl // 2
    bf, f32 = jnp.bfloat16, jnp.float32
    vmem = pl.BlockSpec(memory_space=pltpu.VMEM)
    hbm = pl.BlockSpec(memory_space=pl.ANY)
    dma = pltpu.SemaphoreType.DMA
    out = pl.pallas_call(
        functools.partial(fused_kernel, n_grp, n_mdl, n_k, n_head),
        out_shape=(
            jax.ShapeDtypeStruct((rows, d), bf),
            jax.ShapeDtypeStruct((rows, d), bf),
            jax.ShapeDtypeStruct((lengths.shape[0], 1), f32),
        ),
        in_specs=[vmem] * 6 + [hbm] * 8 + [vmem] * 2,
        out_specs=(vmem, vmem, vmem),
        scratch_shapes=[
            pltpu.VMEM((2, n_mdl * 16, d // 4), bf),
            pltpu.VMEM((2, n_k, tg, kc), bf),
            pltpu.VMEM((2, n_mdl, tg, cb), bf),
            pltpu.VMEM((tg, ff), f32),
            pltpu.VMEM((tg, ff), f32),
            pltpu.VMEM((tg, ff), bf),
            pltpu.VMEM((2 * DEPTH, kc, ff), bf),
            pltpu.VMEM((n_mdl, ff, cb), bf),
            pltpu.VMEM((2, n_head, hc, d), bf),
            pltpu.VMEM((2, n_mdl - 1, tg, cb), bf),
            pltpu.VMEM((2, n_mdl, tg, cb), bf),
            pltpu.VMEM((2, tg, cb), f32),
            pltpu.VMEM((2, n_grp * n_mdl, tg, cb), bf),
            pltpu.VMEM((tokens, d), bf),
            pltpu.VMEM((2, 8, tokens), f32),
            pltpu.VMEM((n_mdl, 8, tokens), f32),
            pltpu.VMEM((n_grp, 8, tokens), f32),
            dma((2 * DEPTH,)), dma((n_mdl,)), dma((2, n_head)),
            dma((2, n_mdl - 1)), dma((2, n_mdl)), dma((2, n_mdl - 1)), dma((2, n_mdl)),
            dma((2, n_z - 1)), dma((2, n_z, n_grp - 1)), dma((2, n_grp, n_z)), dma((2, n_grp * n_mdl)),
            dma((n_mdl - 1,)), dma((n_mdl,)), dma((n_grp - 1,)), dma((n_grp,)),
        ],
        compiler_params=pltpu.CompilerParams(
            collective_id=0, has_side_effects=True, vmem_limit_bytes=VMEM_LIMIT
        ),
    )(
        pol_hidden.reshape(16, d // 4), ref_hidden.reshape(16, d // 4),
        pol_mlp_gain.reshape(1, d), ref_mlp_gain.reshape(1, d),
        pol_final_gain.reshape(1, d), ref_final_gain.reshape(1, d),
        pol_gate, pol_up, pol_down, ref_gate, ref_up, ref_down, pol_head, ref_head,
        token_ids.reshape(1, tokens), lengths.reshape(1, -1),
    )
    return (out[0], out[1], out[2].reshape(-1))


def solution(mesh):
    placed = (
        P(("grp", "mdl"), None),
        P(("grp", "mdl"), None),
        P(),
        P(),
        P(),
        P(),
        P(None, "mdl"),
        P(None, "mdl"),
        P("mdl", None),
        P(None, "mdl"),
        P(None, "mdl"),
        P("mdl", None),
        P(("grp", "mdl"), None),
        P(("grp", "mdl"), None),
        P(),
        P(),
    )

    def local(*args):
        rows, d = args[0].shape
        ff, voc, tokens = args[6].shape[1], args[12].shape[0], args[14].shape[0]
        if fits(mesh.shape["grp"], mesh.shape["mdl"], rows, d, ff, voc, tokens):
            return fused(*args)
        return per_device(*args)

    return jax.shard_map(
        local,
        mesh=mesh,
        in_specs=placed,
        out_specs=(P(("grp", "mdl"), None), P(("grp", "mdl"), None), P()),
        check_vma=False,
    )
```

```python
import functools

import jax
import jax.numpy as jnp
from jax import lax
from jax.experimental import pallas as pl
from jax.experimental.pallas import tpu as pltpu
from jax.sharding import PartitionSpec as P

MESH = pl.DeviceIdType.MESH
DEPTH = 4
EARLY = 2
VMEM_LIMIT = 62 * 1024 * 1024


def rms_rows(rows, gain):
    values = rows.astype(jnp.float32)
    scale = lax.rsqrt(jnp.mean(values * values, axis=-1, keepdims=True) + 1e-05)
    return (values * scale * gain.astype(jnp.float32)).astype(jnp.bfloat16)


def mlp_hidden(piece, gain, w_gate, w_up):
    normed = rms_rows(piece, gain)
    gate = jnp.dot(normed, w_gate, preferred_element_type=jnp.float32)
    upper = jnp.dot(normed, w_up, preferred_element_type=jnp.float32)
    return (jax.nn.silu(gate) * upper).astype(jnp.bfloat16)


def vocab_terms(token_rows, head_rows, targets, vocab):
    logits = jnp.einsum("td,vd->tv", token_rows, head_rows, preferred_element_type=jnp.float32)
    peak = jnp.max(logits, axis=1)
    total = jnp.sum(jnp.exp(logits - peak[:, None]), axis=1)
    target = jnp.sum(jnp.where(targets[:, None] == vocab[None, :], logits, 0.0), axis=1)
    return (peak, total, target)


def rollout_totals(log_ratio, positions, lengths):
    order = jnp.arange(lengths.shape[0], dtype=jnp.int32)
    ends = jnp.sum(jnp.where(order[None, :] <= order[:, None], lengths[None, :], 0), axis=1)
    owner = jnp.sum((positions[:, None] >= ends[None, :]).astype(jnp.int32), axis=1)
    onehot = (owner[:, None] == jnp.arange(lengths.shape[0], dtype=jnp.int32)[None, :]).astype(
        jnp.float32
    )
    return jnp.sum(log_ratio[:, None] * onehot, axis=0)


def per_device(
    pol_hidden,
    ref_hidden,
    pol_mlp_gain,
    ref_mlp_gain,
    pol_final_gain,
    ref_final_gain,
    pol_gate,
    pol_up,
    pol_down,
    ref_gate,
    ref_up,
    ref_down,
    pol_head,
    ref_head,
    token_ids,
    lengths,
):
    results = []
    models = (
        (pol_hidden, pol_mlp_gain, pol_gate, pol_up, pol_down),
        (ref_hidden, ref_mlp_gain, ref_gate, ref_up, ref_down),
    )
    for hidden_in, gain, w_gate, w_up, w_down in models:

        def expand(piece, start, gain=gain, w_gate=w_gate, w_up=w_up):
            return mlp_hidden(piece, gain, w_gate, w_up)

        hidden = expand(lax.all_gather(hidden_in, "mdl", axis=0, tiled=True), jnp.int32(0))

        def project(start, count, hidden=hidden, w_down=w_down):
            return jnp.dot(hidden, w_down, preferred_element_type=jnp.float32)

        mixed = lax.psum_scatter(
            project(jnp.int32(0), hidden_in.shape[0] * lax.axis_size("mdl")),
            "mdl",
            scatter_dimension=0,
            tiled=True,
        )
        results.append((hidden_in.astype(jnp.float32) + mixed).astype(jnp.bfloat16))
    finals = [rms_rows(results[0], pol_final_gain), rms_rows(results[1], ref_final_gain)]
    voc_dev = pol_head.shape[0]
    members = lax.axis_size("mdl")
    group = lax.axis_index("grp")
    member = lax.axis_index("mdl")
    pol_rows, ref_rows = (
        lax.all_gather(finals[0], ("grp", "mdl"), axis=0, tiled=True),
        lax.all_gather(finals[1], ("grp", "mdl"), axis=0, tiled=True),
    )
    positions = jnp.arange(pol_rows.shape[0], dtype=jnp.int32)
    vocab = (group * members + member) * voc_dev + jnp.arange(voc_dev, dtype=jnp.int32)
    pol_terms = vocab_terms(pol_rows, pol_head, token_ids, vocab)
    ref_terms = vocab_terms(ref_rows, ref_head, token_ids, vocab)
    peaks = lax.pmax((pol_terms[0], ref_terms[0]), ("grp", "mdl"))
    sums = lax.psum(
        (
            pol_terms[1] * jnp.exp(pol_terms[0] - peaks[0]),
            pol_terms[2],
            ref_terms[1] * jnp.exp(ref_terms[0] - peaks[1]),
            ref_terms[2],
        ),
        ("grp", "mdl"),
    )
    pol_logp = sums[1] - peaks[0] - jnp.log(sums[0])
    ref_logp = sums[3] - peaks[1] - jnp.log(sums[2])
    rollout_ratio = rollout_totals(pol_logp - ref_logp, positions, lengths)
    return (results[0], results[1], rollout_ratio)


def fused_kernel(
    n_grp, n_mdl, n_k, n_head,
    hidden, gains,
    pol_gate, pol_up, pol_down, ref_gate, ref_up, ref_down,
    pol_head, ref_head, ids, lengths,
    pol_out, ref_out, ratio_out,
    hid, xs, xraw, acc_g, acc_u, hbuf, ring_a, ring_b, heads,
    rs_send, rs_recv, own_part, yall, fin, st_send, st1, st2,
    sem_a, sem_b, sem_h, hs_sem, hr_sem, rss_sem, rsr_sem,
    zs_sem, xs_sem, cs_sem, yr_sem, s1s_sem, s1r_sem, s2s_sem, s2r_sem,
):
    g = lax.axis_index("grp")
    m = lax.axis_index("mdl")
    n_z = n_mdl // 2
    tg = xs.shape[2]
    kc = xs.shape[3]
    d = pol_gate.shape[1]
    cb = d // n_mdl
    quarter = d // 4
    hc = pol_head.shape[0] // n_head
    gates, ups, downs = (pol_gate, ref_gate), (pol_up, ref_up), (pol_down, ref_down)
    head_refs = (pol_head, ref_head)
    hids = (hidden.at[0:16], hidden.at[16:32])
    outs = (pol_out, ref_out)

    def copy_a(mod, k):
        slot = lax.rem(k, DEPTH) * 2
        cols = pl.ds(pl.multiple_of(k * kc, kc), kc)
        return (
            pltpu.make_async_copy(gates[mod].at[:, cols], ring_a.at[slot], sem_a.at[slot]),
            pltpu.make_async_copy(ups[mod].at[:, cols], ring_a.at[slot + 1], sem_a.at[slot + 1]),
        )

    def start_a(mod, k):
        for c in copy_a(mod, k):
            c.start()

    def copy_b(mod, j):
        peer = lax.rem(m + 1 + j, n_mdl)
        cols = pl.ds(pl.multiple_of(peer * cb, cb), cb)
        return pltpu.make_async_copy(downs[mod].at[:, cols], ring_b.at[j], sem_b.at[j])

    def copy_h(mod, c):
        rows = pl.ds(pl.multiple_of(c * hc, hc), hc)
        return pltpu.make_async_copy(head_refs[mod].at[rows, :], heads.at[mod, c], sem_h.at[mod, c])

    def remote(src, dst, ssem, rsem, dg, dm):
        return pltpu.make_async_remote_copy(
            src_ref=src, dst_ref=dst, send_sem=ssem, recv_sem=rsem,
            device_id=(dg, dm), device_id_type=MESH,
        )

    def loop(n, body, start=0):
        def step(i, carry):
            body(i)
            return carry

        lax.fori_loop(start, n, step, 0)

    loop(DEPTH, lambda k: start_a(0, k))
    loop(n_mdl, lambda j: copy_b(0, j).start())
    loop(EARLY, lambda c: copy_h(0, c).start())

    barrier = pltpu.get_barrier_semaphore()
    for i in range(1, n_mdl):
        pl.semaphore_signal(barrier, inc=1, device_id=(g, lax.rem(m + i, n_mdl)), device_id_type=MESH)
    for i in range(1, n_grp):
        pl.semaphore_signal(barrier, inc=1, device_id=(lax.rem(g + i, n_grp), m), device_id_type=MESH)
    pl.semaphore_wait(barrier, n_mdl + n_grp - 2)

    def hid_rows(mod, who):
        return hid.at[mod, pl.ds(pl.multiple_of(who * 16, 16), 16)]

    def hid_copy(mod, i, sender):
        peer = lax.rem(m + 1 + i, n_mdl)
        return remote(hids[mod], hid_rows(mod, sender), hs_sem.at[mod, i], hr_sem.at[mod, sender], g, peer)

    for mod in (0, 1):
        loop(n_mdl - 1, lambda i, mod=mod: hid_copy(mod, i, m).start())
        hid[mod, pl.ds(pl.multiple_of(m * 16, 16), 16)] = hids[mod][...]

    def normed_input(mod):
        loop(n_mdl - 1, lambda i: hid_copy(mod, i, lax.rem(m + 1 + i, n_mdl)).wait_recv())
        stacked = hid[mod]
        t = lax.broadcasted_iota(jnp.int32, (tg, n_mdl * 16), 0)
        r = lax.broadcasted_iota(jnp.int32, (tg, n_mdl * 16), 1)
        parts = []
        total = jnp.zeros((tg, 1), jnp.float32)
        for q in range(4):
            pick = (r == t * 4 + q).astype(jnp.bfloat16)
            part = jnp.dot(pick, stacked, preferred_element_type=jnp.float32)
            total += jnp.sum(part * part, axis=1, keepdims=True)
            parts.append(part)
        scale = lax.rsqrt(total / d + 1e-05)
        for q in range(4):
            gain = gains[:, mod * d + q * quarter:mod * d + (q + 1) * quarter]
            normed = (parts[q] * scale * gain).astype(jnp.bfloat16)
            raw = parts[q].astype(jnp.bfloat16)
            for b in range(quarter // kc):
                xs[mod, q * (quarter // kc) + b] = normed[:, b * kc:(b + 1) * kc]
            for b in range(quarter // cb):
                xraw[mod, q * (quarter // cb) + b] = raw[:, b * cb:(b + 1) * cb]

    def expand_step(mod, k, first):
        for c in copy_a(mod, k):
            c.wait()
        slot = lax.rem(k, DEPTH) * 2
        rows = xs[mod, k]
        dims = (((1,), (1,)), ((), ()))
        acc_g[...] += lax.dot_general(rows, ring_a[slot], dims, preferred_element_type=jnp.float32)
        acc_u[...] += lax.dot_general(rows, ring_a[slot + 1], dims, preferred_element_type=jnp.float32)

    def expand(mod):
        acc_g[...] = jnp.zeros_like(acc_g)
        acc_u[...] = jnp.zeros_like(acc_u)

        def early(k):
            expand_step(mod, k, None)
            start_a(mod, k + DEPTH)

        loop(n_k - DEPTH, early)

        def late(k):
            expand_step(mod, k, None)
            if mod == 0:
                start_a(1, k - (n_k - DEPTH))

        loop(n_k, late, n_k - DEPTH)
        gate = acc_g[...]
        hbuf[...] = (gate / (1.0 + jnp.exp(-gate)) * acc_u[...]).astype(jnp.bfloat16)

    def rs_copy(mod, i, sender):
        peer = lax.rem(m + 1 + i, n_mdl)
        return remote(rs_send.at[mod, i], rs_recv.at[mod, sender], rss_sem.at[mod, i],
                      rsr_sem.at[mod, sender], g, peer)

    def project(mod):
        def part(j):
            copy_b(mod, j).wait()
            return jnp.dot(hbuf[...], ring_b[j], preferred_element_type=jnp.float32)

        def step(j):
            rs_send[mod, j] = part(j).astype(jnp.bfloat16)
            rs_copy(mod, j, m).start()
            if mod == 0:
                copy_b(1, j).start()

        loop(n_mdl - 1, step)
        own_part[mod] = part(n_mdl - 1)
        if mod == 0:
            copy_b(1, n_mdl - 1).start()

    core = lax.rem(m, 2)
    sibling = m + 1 - 2 * core
    me = g * n_mdl + m

    def z_peer(i):
        return lax.rem(m + 2 * i, n_mdl)

    def z_copy(mod, i, block):
        return remote(yall.at[mod, block], yall.at[mod, block], zs_sem.at[mod, i], yr_sem.at[mod, block],
                      g, z_peer(i + 1))

    def x_copy(mod, zi, i, block):
        return remote(yall.at[mod, block], yall.at[mod, block], xs_sem.at[mod, zi, i], yr_sem.at[mod, block],
                      lax.rem(g + 1 + i, n_grp), m)

    def c_copy(mod, gi, zi, block):
        return remote(yall.at[mod, block], yall.at[mod, block], cs_sem.at[mod, gi, zi], yr_sem.at[mod, block],
                      g, sibling)

    def block_of(gi, zi):
        return lax.rem(g + gi, n_grp) * n_mdl + z_peer(zi)

    def finish(mod):
        total = own_part[mod] + xraw[mod, m].astype(jnp.float32)
        for i in range(n_mdl - 1):
            sender = lax.rem(m + 1 + i, n_mdl)
            rs_copy(mod, i, sender).wait_recv()
            total += rs_recv[mod, sender].astype(jnp.float32)
        yall[mod, me] = total.astype(jnp.bfloat16)
        loop(n_z - 1, lambda i: z_copy(mod, i, me).start())
        loop(n_grp - 1, lambda i: x_copy(mod, 0, i, me).start())
        c_copy(mod, 0, 0, me).start()

    def spread_grp(mod):
        def step(zi):
            block = block_of(0, zi)
            z_copy(mod, zi - 1, block).wait_recv()
            loop(n_grp - 1, lambda i: x_copy(mod, zi, i, block).start())
            c_copy(mod, 0, zi, block).start()

        loop(n_z, step, 1)

    def spread_core(mod):
        def per_z(zi):
            def per_g(gi):
                block = block_of(gi, zi)
                x_copy(mod, zi, gi - 1, block).wait_recv()
                c_copy(mod, gi, zi, block).start()

            loop(n_grp, per_g, 1)

        loop(n_z, per_z)

    def arrive(mod):
        def per_z(zi):
            def per_g(gi):
                block = lax.rem(g + gi, n_grp) * n_mdl + lax.rem(sibling + 2 * zi, n_mdl)
                c_copy(mod, gi, zi, block).wait_recv()

            loop(n_grp, per_g)

        loop(n_z, per_z)

    def final_norm(mod):
        for gi in range(n_grp):
            total = jnp.zeros((tg, 1), jnp.float32)
            for b in range(n_mdl):
                y = yall[mod, gi * n_mdl + b].astype(jnp.float32)
                total += jnp.sum(y * y, axis=1, keepdims=True)
            scale = lax.rsqrt(total / d + 1e-05)
            for b in range(n_mdl):
                y = yall[mod, gi * n_mdl + b].astype(jnp.float32)
                gain = gains[:, (2 + mod) * d + b * cb:(2 + mod) * d + (b + 1) * cb]
                fin[gi * tg:(gi + 1) * tg, b * cb:(b + 1) * cb] = (y * scale * gain).astype(jnp.bfloat16)

    def write_out(mod):
        rows = outs[mod].shape[0]
        r = lax.broadcasted_iota(jnp.int32, (8, tg), 0)
        t = lax.broadcasted_iota(jnp.int32, (8, tg), 1)
        pick = (t == m * rows + r).astype(jnp.bfloat16)
        for b in range(n_mdl):
            got = jnp.dot(pick, yall[mod, g * n_mdl + b], preferred_element_type=jnp.float32)
            outs[mod][:, b * cb:(b + 1) * cb] = got[:rows].astype(jnp.bfloat16)

    tokens = fin.shape[0]
    first_word = me * (hc * n_head)

    def head_step(mod, c, carry):
        peak, total, target = carry
        copy_h(mod, c).wait()
        logits = lax.dot_general(heads[mod, c], fin[...], (((1,), (1,)), ((), ())),
                                 preferred_element_type=jnp.float32)
        higher = jnp.maximum(peak, jnp.max(logits, axis=0, keepdims=True))
        total = total * jnp.exp(peak - higher) + jnp.sum(jnp.exp(logits - higher), axis=0, keepdims=True)
        word = lax.broadcasted_iota(jnp.int32, (hc, tokens), 0) + (first_word + c * hc)
        target = target + jnp.sum(jnp.where(word == ids[...], logits, 0.0), axis=0, keepdims=True)
        return (higher, total, target)

    def head_part(mod, lo, hi, carry):
        return lax.fori_loop(lo, hi, lambda c, carry: head_step(mod, c, carry), carry)

    def nothing():
        return (
            jnp.full((1, tokens), -3.0e38, jnp.float32),
            jnp.zeros((1, tokens), jnp.float32),
            jnp.zeros((1, tokens), jnp.float32),
        )

    normed_input(0)
    expand(0)
    project(0)
    normed_input(1)
    loop(n_head, lambda c: copy_h(0, c).start(), EARLY)
    expand(1)
    loop(n_head, lambda c: copy_h(1, c).start())
    finish(0)
    project(1)
    spread_grp(0)
    spread_core(0)
    finish(1)
    arrive(0)
    final_norm(0)
    spread_grp(1)
    stats = head_part(0, 0, 3, nothing())
    spread_core(1)
    pol = head_part(0, 3, n_head, stats)
    write_out(0)
    arrive(1)
    final_norm(1)
    ref = head_part(1, 0, n_head, nothing())

    for row, value in enumerate(pol + ref):
        st_send[0, row:row + 1, :] = value
        st1[m, row:row + 1, :] = value

    def s1_copy(i, sender):
        return remote(st_send.at[0], st1.at[sender], s1s_sem.at[i], s1r_sem.at[sender],
                      g, lax.rem(m + 1 + i, n_mdl))

    def s2_copy(i, sender):
        return remote(st_send.at[1], st2.at[sender], s2s_sem.at[i], s2r_sem.at[sender],
                      lax.rem(g + 1 + i, n_grp), m)

    def merge(ref, count):
        merged = []
        for base in (0, 3):
            peaks = [ref[i, base:base + 1, :] for i in range(count)]
            peak = functools.reduce(jnp.maximum, peaks)
            total = jnp.zeros((1, tokens), jnp.float32)
            target = jnp.zeros((1, tokens), jnp.float32)
            for i in range(count):
                total += ref[i, base + 1:base + 2, :] * jnp.exp(peaks[i] - peak)
                target += ref[i, base + 2:base + 3, :]
            merged += [peak, total, target]
        return merged

    loop(n_mdl - 1, lambda i: s1_copy(i, m).start())
    write_out(1)
    loop(n_mdl - 1, lambda i: s1_copy(i, lax.rem(m + 1 + i, n_mdl)).wait_recv())
    for row, value in enumerate(merge(st1, n_mdl)):
        st_send[1, row:row + 1, :] = value
        st2[g, row:row + 1, :] = value
    loop(n_grp - 1, lambda i: s2_copy(i, g).start())

    for mod in (0, 1):
        loop(n_mdl - 1, lambda i, mod=mod: hid_copy(mod, i, m).wait_send())
        loop(n_mdl - 1, lambda i, mod=mod: rs_copy(mod, i, m).wait_send())
        loop(n_z - 1, lambda i, mod=mod: z_copy(mod, i, me).wait_send())

        def sent(zi, mod=mod):
            loop(n_grp - 1, lambda i: x_copy(mod, zi, i, block_of(0, zi)).wait_send())
            loop(n_grp, lambda gi: c_copy(mod, gi, zi, block_of(gi, zi)).wait_send())

        loop(n_z, sent)
    loop(n_mdl - 1, lambda i: s1_copy(i, m).wait_send())

    n_roll = ratio_out.shape[1]
    row = lax.broadcasted_iota(jnp.int32, (n_roll, n_roll), 0)
    col = lax.broadcasted_iota(jnp.int32, (n_roll, n_roll), 1)
    size = jnp.broadcast_to(lengths[...].astype(jnp.float32), (n_roll, n_roll))
    ends = jnp.sum(jnp.where(col <= row, size, 0.0), axis=1, keepdims=True)
    starts = jnp.sum(jnp.where(col < row, size, 0.0), axis=1, keepdims=True)
    position = lax.broadcasted_iota(jnp.int32, (n_roll, tokens), 1).astype(jnp.float32)
    held = jnp.where((position >= starts) & (position < ends), 1.0, 0.0)

    loop(n_grp - 1, lambda i: s2_copy(i, lax.rem(g + 1 + i, n_grp)).wait_recv())
    pp, ps, pt, rp, rt, rg = merge(st2, n_grp)
    log_ratio = (pt - pp - jnp.log(ps)) - (rg - rp - jnp.log(rt))
    ratio = jnp.sum(held * log_ratio, axis=1, keepdims=True)
    ratio_out[...] = jnp.sum(jnp.where(row == col, ratio, 0.0), axis=0, keepdims=True)
    loop(n_grp - 1, lambda i: s2_copy(i, g).wait_send())


def pick_head_chunks(voc):
    for n in (5, 4, 8, 10):
        if voc % n == 0 and (voc // n) % 16 == 0:
            return n
    return 0


def fits(n_grp, n_mdl, rows, d, ff, voc, tokens):
    if rows != 4 or n_mdl % 2 or n_mdl < 4 or n_grp < 2 or tokens > 128 or not pick_head_chunks(voc):
        return False
    if d % (4 * n_mdl) or (d // n_mdl) % 128 or d % 32 or (d // 8) % 128 or (d // 4) % (d // n_mdl) or ff % 16:
        return False
    need = 2 * (2 * DEPTH * (d // 8) * ff + ff * d + 2 * voc * d + 6 * tokens * d)
    return need < VMEM_LIMIT


def fused(
    pol_hidden, ref_hidden, pol_mlp_gain, ref_mlp_gain, pol_final_gain, ref_final_gain,
    pol_gate, pol_up, pol_down, ref_gate, ref_up, ref_down, pol_head, ref_head, token_ids, lengths,
):
    n_grp, n_mdl = lax.axis_size("grp"), lax.axis_size("mdl")
    rows, d = pol_hidden.shape
    ff, voc, tokens = pol_gate.shape[1], pol_head.shape[0], token_ids.shape[0]
    n_k, n_head = 8, pick_head_chunks(voc)
    tg, kc, cb, hc = rows * n_mdl, d // n_k, d // n_mdl, voc // n_head
    n_z = n_mdl // 2
    bf, f32 = jnp.bfloat16, jnp.float32
    vmem = pl.BlockSpec(memory_space=pltpu.VMEM)
    hbm = pl.BlockSpec(memory_space=pl.ANY)
    dma = pltpu.SemaphoreType.DMA
    out = pl.pallas_call(
        functools.partial(fused_kernel, n_grp, n_mdl, n_k, n_head),
        out_shape=(
            jax.ShapeDtypeStruct((rows, d), bf),
            jax.ShapeDtypeStruct((rows, d), bf),
            jax.ShapeDtypeStruct((1, lengths.shape[0]), f32),
        ),
        in_specs=[vmem] * 2 + [hbm] * 8 + [vmem] * 2,
        out_specs=(vmem, vmem, vmem),
        scratch_shapes=[
            pltpu.VMEM((2, n_mdl * 16, d // 4), bf),
            pltpu.VMEM((2, n_k, tg, kc), bf),
            pltpu.VMEM((2, n_mdl, tg, cb), bf),
            pltpu.VMEM((tg, ff), f32),
            pltpu.VMEM((tg, ff), f32),
            pltpu.VMEM((tg, ff), bf),
            pltpu.VMEM((2 * DEPTH, ff, kc), bf),
            pltpu.VMEM((n_mdl, ff, cb), bf),
            pltpu.VMEM((2, n_head, hc, d), bf),
            pltpu.VMEM((2, n_mdl - 1, tg, cb), bf),
            pltpu.VMEM((2, n_mdl, tg, cb), bf),
            pltpu.VMEM((2, tg, cb), f32),
            pltpu.VMEM((2, n_grp * n_mdl, tg, cb), bf),
            pltpu.VMEM((tokens, d), bf),
            pltpu.VMEM((2, 8, tokens), f32),
            pltpu.VMEM((n_mdl, 8, tokens), f32),
            pltpu.VMEM((n_grp, 8, tokens), f32),
            dma((2 * DEPTH,)), dma((n_mdl,)), dma((2, n_head)),
            dma((2, n_mdl - 1)), dma((2, n_mdl)), dma((2, n_mdl - 1)), dma((2, n_mdl)),
            dma((2, n_z - 1)), dma((2, n_z, n_grp - 1)), dma((2, n_grp, n_z)), dma((2, n_grp * n_mdl)),
            dma((n_mdl - 1,)), dma((n_mdl,)), dma((n_grp - 1,)), dma((n_grp,)),
        ],
        compiler_params=pltpu.CompilerParams(
            collective_id=0, has_side_effects=True, vmem_limit_bytes=VMEM_LIMIT
        ),
    )(
        jnp.concatenate([pol_hidden, ref_hidden]).reshape(32, d // 4),
        jnp.concatenate([pol_mlp_gain, ref_mlp_gain, pol_final_gain, ref_final_gain]).astype(f32).reshape(1, 4 * d),
        pol_gate.T, pol_up.T, pol_down, ref_gate.T, ref_up.T, ref_down, pol_head, ref_head,
        token_ids.reshape(1, tokens), lengths.reshape(1, -1),
    )
    return (out[0], out[1], out[2].reshape(-1))


def solution(mesh):
    placed = (
        P(("grp", "mdl"), None),
        P(("grp", "mdl"), None),
        P(),
        P(),
        P(),
        P(),
        P(None, "mdl"),
        P(None, "mdl"),
        P("mdl", None),
        P(None, "mdl"),
        P(None, "mdl"),
        P("mdl", None),
        P(("grp", "mdl"), None),
        P(("grp", "mdl"), None),
        P(),
        P(),
    )

    def local(*args):
        rows, d = args[0].shape
        ff, voc, tokens = args[6].shape[1], args[12].shape[0], args[14].shape[0]
        if fits(mesh.shape["grp"], mesh.shape["mdl"], rows, d, ff, voc, tokens):
            return fused(*args)
        return per_device(*args)

    return jax.shard_map(
        local,
        mesh=mesh,
        in_specs=placed,
        out_specs=(P(("grp", "mdl"), None), P(("grp", "mdl"), None), P()),
        check_vma=False,
    )
```
